128 devices in a mesh: gx: 8 (over z, core), yz: 16 (over x, y).
Axes of the slice: x: 4, y: 4, z: 4, core: 2. Of those that a mesh axis runs over, the one named last changes fastest.
Arguments:
- features: bfloat16 [768, 64, 4096], P(('gx', 'yz')), may hold values from -6 to 6
- brick_state: int32 [768], P(('gx', 'yz')), may hold values from -1 to 2, as said below
- neighbor: int32 [768, 6], P(('gx', 'yz')), may hold values from -1 to 11, as said below
- w_first: bfloat16 [27, 64, 64], replicated, may hold values from -0.15625 to 0.15625
- b_first: float32 [64], replicated, may hold values from -3 to 3
- w_second: bfloat16 [27, 64, 64], replicated, may hold values from -0.15625 to 0.15625
- b_second: float32 [64], replicated, may hold values from -3 to 3
Outputs:
- blocks: bfloat16 [768, 64, 4096], P(('gx', 'yz'))
The draws below stay inside these ranges and needn't reach their ends.
Inputs may be any that keep to these rules, and one draw needn't show every extreme that they name: `brick_state`: per slot: -1 empty; 0 occupied and computed by its own region; 1 occupied and lent to the region at yz - 1 of the same slab; 2 lent to the region at yz + 1. A region lends at most 1 bricks to each side, and the bricks it computes (its code-0 bricks and those lent to it) number at most 4; both bounds are reached in every draw, and some region has all 6 slots occupied. `neighbor`: per slot and face (x-, x+, y-, y+, z-, z+): -1 if the slot is empty or no occupied brick touches that face; k < 6 names slot k of the same region; k >= 6 names slot k - 6 of the adjacent region across that face (gx - 1, gx + 1, yz - 1, yz + 1 for the four side faces; z faces never leave the region). Entries point only at occupied slots and adjacency is symmetric.
All inputs are finite; a program needn't handle non-finite values.
Results may differ from the reference program's by a relative error of at most 0.0049.
Values may be sent and summed in bfloat16 or wider, within the bound.
A program may use at most 192 MiB of HBM per device.

```python
import jax
import jax.numpy as jnp
from jax import lax

CH = 64
EDGE = 16
B_DEV = 6
LEND = 1
HOLD = 4
VOXELS = 4096
BRICKS = 768
N_GX = 8
N_YZ = 16


def brick_plan(key):
    regions = N_GX * N_YZ
    height_bricks = B_DEV // 2
    positions_all = 4 * height_bricks
    key_list = jax.random.split(key, 4)
    shift_phase = jax.random.randint(key_list[0], (N_GX,), 0, 3)
    columns = jnp.arange(N_YZ, dtype=jnp.int32)
    crowded = ((columns[None, :] + shift_phase[:, None]) % 3 == 0).reshape(regions)
    has_left = jnp.tile(columns > 0, N_GX)
    has_right = jnp.tile(columns < N_YZ - 1, N_GX)
    missing = (~has_left).astype(jnp.int32) + (~has_right).astype(jnp.int32)
    light_count = jax.random.randint(key_list[1], (regions,), 1, HOLD - LEND + 1)
    brick_count = jnp.where(crowded, B_DEV - LEND * missing, light_count)
    slot_ranks = jax.vmap(lambda part_key: jax.random.permutation(part_key, B_DEV))(jax.random.split(key_list[2], regions)).astype(jnp.int32)
    spot_order = jax.vmap(lambda part_key: jax.random.permutation(part_key, positions_all))(jax.random.split(key_list[3], regions)).astype(jnp.int32)
    occupied = slot_ranks < brick_count[:, None]
    to_left = crowded[:, None] & has_left[:, None] & (slot_ranks < LEND)
    to_right = crowded[:, None] & has_right[:, None] & (slot_ranks >= LEND) & (slot_ranks < 2 * LEND)
    slot_codes = jnp.where(occupied, jnp.where(to_left, 1, jnp.where(to_right, 2, 0)), -1)
    position = jnp.where(occupied, jnp.take_along_axis(spot_order, slot_ranks, axis=1), -1)
    slot_numbers = jnp.arange(B_DEV, dtype=jnp.int32)
    slot_at = jnp.max(jnp.where(position[:, :, None] == jnp.arange(positions_all, dtype=jnp.int32)[None, None, :], slot_numbers[None, :, None], -1), axis=1)
    coord_x = position // (2 * height_bricks)
    coord_y = position // height_bricks % 2
    coord_z = position % height_bricks
    region_index = jnp.arange(regions, dtype=jnp.int32)[:, None]
    slab_index = region_index // N_YZ
    strip_index = region_index % N_YZ
    moves = ((-1, 0, 0), (1, 0, 0), (0, -1, 0), (0, 1, 0), (0, 0, -1), (0, 0, 1))
    columns_out = []
    for move_x, move_y, move_z in moves:
        next_x = coord_x + move_x
        next_y = coord_y + move_y
        next_z = coord_z + move_z
        region_x = slab_index + jnp.where(next_x < 0, -1, jnp.where(next_x > 1, 1, 0))
        region_y = strip_index + jnp.where(next_y < 0, -1, jnp.where(next_y > 1, 1, 0))
        inside = (region_x >= 0) & (region_x < N_GX) & (region_y >= 0) & (region_y < N_YZ) & (next_z >= 0) & (next_z < height_bricks)
        target = jnp.clip(region_x, 0, N_GX - 1) * N_YZ + jnp.clip(region_y, 0, N_YZ - 1)
        target_spot = next_x % 2 * (2 * height_bricks) + next_y % 2 * height_bricks + jnp.clip(next_z, 0, height_bricks - 1)
        found = slot_at[target, target_spot]
        value = jnp.where(target != region_index, found + B_DEV, found)
        valid = inside & occupied & (found >= 0)
        columns_out.append(jnp.where(valid, value, -1))
    table = jnp.stack(columns_out, axis=-1).reshape(regions * B_DEV, 6)
    return (slot_codes.reshape(regions * B_DEV).astype(jnp.int32), table.astype(jnp.int32))


def draw_brick_state(key, part):
    slot_codes, table = brick_plan(key)
    return slot_codes


def draw_neighbor(key, part):
    slot_codes, table = brick_plan(key)
    return table


def level_of(key, shape, shards, least, largest):
    loudness = 1.0
    for dim, shards_of in shards:
        heights = jax.random.uniform(jax.random.fold_in(jax.random.fold_in(key, 6), dim), (shards_of,), jnp.float32, least / len(shards), largest / len(shards))
        loudness = loudness * jnp.repeat(jnp.exp(heights), shape[dim] // shards_of).reshape((-1,) + (1,) * (len(shape) - 1 - dim))
    return loudness


def bell_draw(key, shape, scale, bound, cuts=(), kind=jnp.bfloat16):
    level = level_of(key, shape, cuts, -0.22, 0.18) if cuts else 1.0
    entries = jax.random.normal(key, shape, jnp.float32) * scale * level
    return jnp.minimum(jnp.maximum(entries, -bound), bound).astype(kind)


def setup_inputs(seed: int = 0) -> dict:
    key_of = jax.random.split(jax.random.key(seed), 8)
    return {
        "features": bell_draw(key_of[0], (BRICKS, CH, VOXELS), 1.0, 6.0, ((0, 128),)),
        "brick_state": draw_brick_state(jax.random.fold_in(key_of[7], 71), 0),
        "neighbor": draw_neighbor(jax.random.fold_in(key_of[7], 71), 0),
        "w_first": bell_draw(key_of[3], (27, CH, CH), (27 * CH) ** -0.5, 0.15625),
        "b_first": bell_draw(key_of[4], (CH,), 0.5, 3.0, (), jnp.float32),
        "w_second": bell_draw(key_of[5], (27, CH, CH), (27 * CH) ** -0.5, 0.15625),
        "b_second": bell_draw(key_of[6], (CH,), 0.5, 3.0, (), jnp.float32),
    }


def neighbor_planes(volume, table):
    regions, owned = volume.shape[0], volume.shape[1]
    region_index = jnp.arange(regions, dtype=jnp.int32)[:, None]
    shifts = (-N_YZ, N_YZ, -1, 1, 0, 0)
    planes = [volume[:, :, :, 0], volume[:, :, :, -1], volume[:, :, :, :, 0], volume[:, :, :, :, -1], volume[..., 0], volume[..., -1]]
    result = []
    for face_index in range(6):
        source = planes[face_index ^ 1]
        wanted = table[:, :, face_index]
        remote = wanted >= owned
        source_region = jnp.clip(region_index + jnp.where(remote, shifts[face_index], 0), 0, regions - 1).astype(jnp.int32)
        source_slot = jnp.clip(jnp.where(remote, wanted - owned, wanted), 0, owned - 1).astype(jnp.int32)
        picked = source[source_region, source_slot]
        result.append(jnp.where((wanted >= 0)[:, :, None, None, None], picked, jnp.zeros_like(picked)))
    return result


def convolve_all(volume, planes, weights, bias_row):
    padded = jnp.pad(volume, ((0, 0), (0, 0), (0, 0), (1, 1), (1, 1), (1, 1)))
    padded = padded.at[:, :, :, 0, 1:-1, 1:-1].set(planes[0])
    padded = padded.at[:, :, :, -1, 1:-1, 1:-1].set(planes[1])
    padded = padded.at[:, :, :, 1:-1, 0, 1:-1].set(planes[2])
    padded = padded.at[:, :, :, 1:-1, -1, 1:-1].set(planes[3])
    padded = padded.at[:, :, :, 1:-1, 1:-1, 0].set(planes[4])
    padded = padded.at[:, :, :, 1:-1, 1:-1, -1].set(planes[5])
    wide = weights.astype(jnp.float32)

    def one_region(block):
        block = block.astype(jnp.float32)
        summed = jnp.zeros((block.shape[0], block.shape[1], EDGE, EDGE, EDGE), jnp.float32)
        for step_x in range(3):
            for step_y in range(3):
                for step_z in range(3):
                    window = block[:, :, step_x:step_x + EDGE, step_y:step_y + EDGE, step_z:step_z + EDGE]
                    summed = summed + jnp.einsum("oi,bixyz->boxyz", wide[step_x * 9 + step_y * 3 + step_z], window)
        return summed + bias_row.astype(jnp.float32)[None, :, None, None, None]

    return lax.map(one_region, padded)


def reference(features, brick_state, neighbor, w_first, b_first, w_second, b_second):
    regions = N_GX * N_YZ
    volume = features.reshape(regions, B_DEV, CH, EDGE, EDGE, EDGE)
    table = neighbor.reshape(regions, B_DEV, 6)
    live = (brick_state >= 0).reshape(regions, B_DEV, 1, 1, 1, 1)
    first = convolve_all(volume, neighbor_planes(volume, table), w_first, b_first)
    hidden = jnp.where(live, jax.nn.relu(first), 0.0).astype(jnp.bfloat16)
    second = convolve_all(hidden, neighbor_planes(hidden, table), w_second, b_second)
    branch = second.astype(jnp.bfloat16)
    summed = volume.astype(jnp.float32) + branch.astype(jnp.float32)
    blocks = jnp.where(live, jax.nn.relu(summed), 0.0).astype(jnp.bfloat16)
    return blocks.reshape(regions * B_DEV, CH, EDGE ** 3)
```

```python
import functools

import jax
import jax.numpy as jnp
from jax import lax
from jax.experimental import pallas as pl
from jax.experimental.pallas import tpu as pltpu
from jax.sharding import PartitionSpec as P

EDGE = 16
SLAB = EDGE * EDGE
HALF = SLAB // 2
MESH = pl.DeviceIdType.MESH
VMEM = pltpu.VMEM
LIMIT = 60 * 2**20


def lanes(rows):
    return lax.broadcasted_iota(jnp.int32, (rows, HALF), 1)


def turn(values, shift):
    shift = shift % HALF
    return values if shift == 0 else pltpu.roll(values, shift, axis=1)


def gather_row(plane, slab_half, x, source_lane):
    place = (x % 8) * EDGE
    lane = lanes(plane.shape[0])
    inside = (lane >= place) & (lane < place + EDGE)
    return jnp.where(inside, turn(slab_half, place - source_lane), plane)


def exchange_body(extract, source, *refs):
    if extract:
        halo_x, halo_y, planes_out, staged, planes, load_sem, send_sem, recv_sem, keep_sem = refs
    else:
        planes, halo_x, halo_y, send_sem, recv_sem = refs
    channels = source.shape[1]
    bricks = source.shape[0]
    n_x, n_y = lax.axis_size("gx"), lax.axis_size("yz")
    gx, yz = lax.axis_index("gx"), lax.axis_index("yz")
    x_up = (lax.rem(gx + 1, n_x), yz)
    x_down = (lax.rem(gx + n_x - 1, n_x), yz)
    y_up = (gx, lax.rem(yz + 1, n_y))
    y_down = (gx, lax.rem(yz + n_y - 1, n_y))

    if extract:
        load = pltpu.make_async_copy(source, staged, load_sem)
        load.start()
    barrier = pltpu.get_barrier_semaphore()
    for other in (x_up, x_down, y_up, y_down):
        pl.semaphore_signal(barrier, inc=1, device_id=other, device_id_type=MESH)
    pl.semaphore_wait(barrier, 4)

    def send(index, src, dst, other):
        copy = pltpu.make_async_remote_copy(
            src_ref=src,
            dst_ref=dst,
            send_sem=send_sem.at[index],
            recv_sem=recv_sem.at[index],
            device_id=other,
            device_id_type=MESH,
        )
        copy.start()
        return copy

    copies = [
        send(0, source.at[:, :, pl.ds((EDGE - 1) * SLAB, SLAB)], halo_x.at[0], x_up),
        send(1, source.at[:, :, pl.ds(0, SLAB)], halo_x.at[1], x_down),
    ]
    if extract:
        load.wait()

        def one_brick(b, carry):
            for half in range(2):
                low = jnp.zeros((channels, HALF), staged.dtype)
                high = low
                for x in range(half * 8, half * 8 + 8):
                    low = gather_row(low, staged[b, :, x * SLAB : x * SLAB + HALF], x, 0)
                    high = gather_row(
                        high, staged[b, :, x * SLAB + HALF : (x + 1) * SLAB], x, HALF - EDGE
                    )
                planes[0, b, :, half * HALF : (half + 1) * HALF] = low
                planes[1, b, :, half * HALF : (half + 1) * HALF] = high
            return carry

        lax.fori_loop(0, bricks, one_brick, 0)
    copies.append(send(2, planes.at[1], halo_y.at[0], y_up))
    copies.append(send(3, planes.at[0], halo_y.at[1], y_down))
    if extract:
        keep = pltpu.make_async_copy(planes, planes_out, keep_sem)
        keep.start()
        keep.wait()
    for copy in copies:
        copy.wait()


def first_exchange(features):
    bricks, channels, _ = features.shape
    plane = jax.ShapeDtypeStruct((2, bricks, channels, SLAB), features.dtype)
    anywhere = pl.BlockSpec(memory_space=pl.ANY)
    return pl.pallas_call(
        functools.partial(exchange_body, True),
        out_shape=(plane, plane, plane),
        in_specs=[anywhere],
        out_specs=(anywhere, anywhere, anywhere),
        scratch_shapes=[
            VMEM(features.shape, features.dtype),
            VMEM(plane.shape, plane.dtype),
            pltpu.SemaphoreType.DMA,
            pltpu.SemaphoreType.DMA((4,)),
            pltpu.SemaphoreType.DMA((4,)),
            pltpu.SemaphoreType.DMA,
        ],
        compiler_params=pltpu.CompilerParams(
            collective_id=0, has_side_effects=True, vmem_limit_bytes=LIMIT
        ),
        name="exchange_features",
    )(features)


def second_exchange(hidden, planes):
    plane = jax.ShapeDtypeStruct(planes.shape, planes.dtype)
    anywhere = pl.BlockSpec(memory_space=pl.ANY)
    return pl.pallas_call(
        functools.partial(exchange_body, False),
        out_shape=(plane, plane),
        in_specs=[anywhere, anywhere],
        out_specs=(anywhere, anywhere),
        scratch_shapes=[
            pltpu.SemaphoreType.DMA((4,)),
            pltpu.SemaphoreType.DMA((4,)),
        ],
        compiler_params=pltpu.CompilerParams(
            collective_id=1, has_side_effects=True, vmem_limit_bytes=LIMIT
        ),
        name="exchange_hidden",
    )(hidden, planes)


def conv_body(
    last, state, neighbor, values, halo_x, halo_y, own_y, weights, bias, *refs
):
    if last:
        features, out, stacked, matrix, bias_column = refs
    else:
        out, planes_out, stacked, matrix, bias_column = refs
    b = pl.program_id(0)
    bricks, channels = values.shape[0], values.shape[1]
    kind = values.dtype
    lane = lanes(channels)
    z = lane % EDGE
    zero = jnp.zeros((channels, HALF), kind)

    @pl.when(b == 0)
    def _():
        for dy in range(3):
            blocks = [weights[9 * (j // 3) + 3 * dy + j % 3] for j in range(9)]
            rows = pl.ds(dy * channels, channels)
            for pair in range(4):
                matrix[rows, pair * 2 * channels : (pair + 1) * 2 * channels] = jnp.concatenate(
                    blocks[2 * pair : 2 * pair + 2], axis=1
                )
            matrix[rows, 8 * channels : 9 * channels] = blocks[8]
        row = lax.broadcasted_iota(jnp.int32, (channels, channels), 0)
        column = lax.broadcasted_iota(jnp.int32, (channels, channels), 1)
        wide = jnp.broadcast_to(bias[...], (channels, channels))
        one = jnp.sum(jnp.where(row == column, wide, 0.0), axis=1, keepdims=True)
        bias_column[...] = jnp.broadcast_to(one, (channels, HALF))

    def face(index, own, across):
        k = neighbor[b, index]
        here = jnp.clip(k, 0, bricks - 1)
        there = jnp.clip(k - bricks, 0, bricks - 1)
        picked = jnp.where(k < bricks, own(here), across[index % 2, there])
        return jnp.where(k >= 0, picked, jnp.zeros_like(picked))

    def z_shifted(half, below, above):
        down = jnp.where(z == 0, below, turn(half, 1))
        up = jnp.where(z == EDGE - 1, above, turn(half, -1))
        return down, half, up

    def compute():
        def y_face(index):
            plane = face(index, lambda k: own_y[1 - index % 2, k], halo_y)
            a, c = plane[:, :HALF], plane[:, HALF:]
            ra, rc = turn(a, EDGE), turn(c, EDGE)
            before = (jnp.where(lane < EDGE, zero, ra), jnp.where(lane < EDGE, ra, rc))
            ra, rc = turn(a, -EDGE), turn(c, -EDGE)
            edge = lane >= HALF - EDGE
            after = (jnp.where(edge, rc, ra), jnp.where(edge, zero, rc))
            blocks = []
            for left, right in (before, (a, c), after):
                for l, r in zip(z_shifted(left, zero, zero), z_shifted(right, zero, zero)):
                    blocks.append(jnp.concatenate([l, r], axis=1))
            tall = jnp.concatenate(blocks, axis=0)
            dy = 2 * (index % 2)
            return jnp.dot(
                matrix[dy * channels : (dy + 1) * channels, :],
                tall,
                preferred_element_type=jnp.float32,
            )

        low_y, high_y = y_face(2), y_face(3)

        def put(x, a_shifts, c_shifts):
            for dz in range(3):
                rows = pl.ds(dz * channels, channels)
                stacked[x + 1, rows, :HALF] = a_shifts[dz]
                stacked[x + 1, rows, HALF:] = c_shifts[dz]

        for x, index in ((-1, 0), (EDGE, 1)):
            first = (EDGE - 1) * SLAB if index == 0 else 0
            slab = face(index, lambda k, first=first: values[k, :, first : first + SLAB], halo_x)
            put(x, z_shifted(slab[:, :HALF], zero, zero), z_shifted(slab[:, HALF:], zero, zero))

        def z_neighbor(index):
            k = neighbor[b, index]
            return k >= 0, jnp.clip(jnp.where(k >= bricks, k - bricks, k), 0, bricks - 1)

        has_below, below = z_neighbor(4)
        has_above, above = z_neighbor(5)
        for x in range(EDGE):
            shifts = []
            for half in range(2):
                first = x * SLAB + half * HALF
                low = turn(values[below, :, first : first + HALF], 1 - EDGE)
                high = turn(values[above, :, first : first + HALF], EDGE - 1)
                shifts.append(
                    z_shifted(
                        values[b, :, first : first + HALF],
                        jnp.where(has_below, low, zero),
                        jnp.where(has_above, high, zero),
                    )
                )
            put(x, *shifts)

        if not last:
            low_planes, high_planes = [zero, zero], [zero, zero]
        for x in range(EDGE):
            taps = stacked[x : x + 3].reshape(9 * channels, SLAB)
            sums = jnp.dot(matrix[...], taps, preferred_element_type=jnp.float32)
            before, middle, after = (
                sums[i * channels : (i + 1) * channels] for i in range(3)
            )
            quarter = x // 8
            place = (x % 8) * EDGE
            low = turn(low_y[:, quarter * HALF : (quarter + 1) * HALF], -place)
            high = turn(high_y[:, quarter * HALF : (quarter + 1) * HALF], HALF - EDGE - place)
            ra, rc = turn(before[:, :HALF], EDGE), turn(before[:, HALF:], EDGE)
            first = (jnp.where(lane < EDGE, low, ra), jnp.where(lane < EDGE, ra, rc))
            ra, rc = turn(after[:, :HALF], -EDGE), turn(after[:, HALF:], -EDGE)
            edge = lane >= HALF - EDGE
            second = (jnp.where(edge, rc, ra), jnp.where(edge, high, rc))
            for half in range(2):
                span = slice(x * SLAB + half * HALF, x * SLAB + (half + 1) * HALF)
                total = middle[:, half * HALF : (half + 1) * HALF] + first[half]
                total = total + second[half] + bias_column[...]
                if last:
                    branch = total.astype(kind).astype(jnp.float32)
                    total = features[0, :, span].astype(jnp.float32) + branch
                done = jnp.maximum(total, 0.0).astype(kind)
                out[0, :, span] = done
                if not last and half == 0:
                    low_planes[quarter] = gather_row(low_planes[quarter], done, x, 0)
                elif not last:
                    high_planes[quarter] = gather_row(high_planes[quarter], done, x, HALF - EDGE)
        if not last:
            for quarter in range(2):
                span = slice(quarter * HALF, (quarter + 1) * HALF)
                planes_out[0, 0, :, span] = low_planes[quarter]
                planes_out[1, 0, :, span] = high_planes[quarter]

    live = state[b] >= 0

    @pl.when(live)
    def _():
        compute()

    @pl.when(jnp.logical_not(live))
    def _():
        out[...] = jnp.zeros_like(out)
        if not last:
            planes_out[...] = jnp.zeros_like(planes_out)


def conv(last, state, neighbor, values, halo_x, halo_y, own_y, weights, bias, features=None):
    bricks, channels, voxels = values.shape
    kind = values.dtype
    whole = pl.BlockSpec(memory_space=VMEM)
    scalar = pl.BlockSpec(memory_space=pltpu.SMEM)
    brick = pl.BlockSpec((1, channels, voxels), lambda b: (b, 0, 0))
    plane = pl.BlockSpec((2, 1, channels, SLAB), lambda b: (0, b, 0, 0))
    args = [state, neighbor, values, halo_x, halo_y, own_y, weights, bias.reshape(1, channels)]
    in_specs = [scalar, scalar] + [whole] * 6
    out_shape = jax.ShapeDtypeStruct(values.shape, kind)
    out_specs = brick
    if last:
        args.append(features)
        in_specs.append(brick)
    else:
        out_shape = (out_shape, jax.ShapeDtypeStruct((2, bricks, channels, SLAB), kind))
        out_specs = (brick, plane)
    return pl.pallas_call(
        functools.partial(conv_body, last),
        grid=(bricks,),
        out_shape=out_shape,
        in_specs=in_specs,
        out_specs=out_specs,
        scratch_shapes=[
            VMEM((EDGE + 2, 3 * channels, SLAB), kind),
            VMEM((3 * channels, 9 * channels), kind),
            VMEM((channels, HALF), jnp.float32),
        ],
        compiler_params=pltpu.CompilerParams(vmem_limit_bytes=LIMIT),
        name="second_conv" if last else "first_conv",
    )(*args)


def per_device(features, brick_state, neighbor, w_first, b_first, w_second, b_second):
    halo_x, halo_y, own_y = first_exchange(features)
    hidden, planes = conv(
        False, brick_state, neighbor, features, halo_x, halo_y, own_y, w_first, b_first
    )
    halo_x, halo_y = second_exchange(hidden, planes)
    return conv(
        True, brick_state, neighbor, hidden, halo_x, halo_y, planes, w_second, b_second, features
    )


def solution(mesh):
    in_specs = (
        P(("gx", "yz"), None, None),
        P(("gx", "yz")),
        P(("gx", "yz"), None),
        P(),
        P(),
        P(),
        P(),
    )
    out_specs = P(("gx", "yz"), None, None)
    return jax.shard_map(
        per_device, mesh=mesh, in_specs=in_specs, out_specs=out_specs, check_vma=False
    )
```

```python
import jax
import jax.numpy as jnp
from jax import lax
from jax.experimental import pallas as pl
from jax.experimental.pallas import tpu as pltpu
from jax.sharding import PartitionSpec as P

EDGE = 16
SLAB = EDGE * EDGE
HALF = SLAB // 2
MESH = pl.DeviceIdType.MESH
VMEM = pltpu.VMEM
LIMIT = 60 * 2**20


def lanes(rows):
    return lax.broadcasted_iota(jnp.int32, (rows, HALF), 1)


def turn(values, shift):
    shift = shift % HALF
    return values if shift == 0 else pltpu.roll(values, shift, axis=1)


def gather_row(plane, slab_half, x, source_lane):
    place = (x % 8) * EDGE
    lane = lanes(plane.shape[0])
    inside = (lane >= place) & (lane < place + EDGE)
    return jnp.where(inside, turn(slab_half, place - source_lane), plane)


def at_x(x):
    return slice(x * SLAB, (x + 1) * SLAB)


def outer_rows(values, b, planes):
    channels = values.shape[1]
    for half in range(2):
        low = jnp.zeros((channels, HALF), values.dtype)
        high = low
        for x in range(half * 8, half * 8 + 8):
            low = gather_row(low, values[b, :, x * SLAB : x * SLAB + HALF], x, 0)
            high = gather_row(high, values[b, :, x * SLAB + HALF : (x + 1) * SLAB], x, HALF - EDGE)
        planes[0, b, :, half * HALF : (half + 1) * HALF] = low
        planes[1, b, :, half * HALF : (half + 1) * HALF] = high


def z_shifted(half, below, above):
    z = lanes(half.shape[0]) % EDGE
    down = jnp.where(z == 0, below, turn(half, 1))
    up = jnp.where(z == EDGE - 1, above, turn(half, -1))
    return down, half, up


def put(stacked, b, x, left, right):
    channels = left[0].shape[0]
    for dz in range(3):
        rows = slice(dz * channels, (dz + 1) * channels)
        stacked[b, x + 1, rows, :HALF] = left[dz]
        stacked[b, x + 1, rows, HALF:] = right[dz]


def stack_brick(values, neighbor, b, stacked):
    bricks, channels = values.shape[0], values.shape[1]
    zero = jnp.zeros((channels, HALF), values.dtype)

    def z_neighbor(index):
        k = neighbor[b, index]
        return k >= 0, jnp.clip(jnp.where(k >= bricks, k - bricks, k), 0, bricks - 1)

    has_below, below = z_neighbor(4)
    has_above, above = z_neighbor(5)
    for x in range(EDGE):
        shifts = []
        for half in range(2):
            span = slice(x * SLAB + half * HALF, x * SLAB + (half + 1) * HALF)
            low = turn(values[below, :, span], 1 - EDGE)
            high = turn(values[above, :, span], EDGE - 1)
            shifts.append(
                z_shifted(
                    values[b, :, span],
                    jnp.where(has_below, low, zero),
                    jnp.where(has_above, high, zero),
                )
            )
        put(stacked, b, x, *shifts)


def conv_brick(values, halo_x, halo_y, own_y, neighbor, b, stacked, matrix, bias, finish):
    bricks, channels = values.shape[0], values.shape[1]
    lane = lanes(channels)
    zero = jnp.zeros((channels, HALF), values.dtype)
    edge = lane >= HALF - EDGE

    def face(index, own, across):
        k = neighbor[b, index]
        here = jnp.clip(k, 0, bricks - 1)
        there = jnp.clip(k - bricks, 0, bricks - 1)
        picked = jnp.where(k < bricks, own(here), across[index % 2, there])
        return jnp.where(k >= 0, picked, jnp.zeros_like(picked))

    def y_face(index):
        plane = face(index, lambda k: own_y[1 - index % 2, k], halo_y)
        a, c = plane[:, :HALF], plane[:, HALF:]
        ra, rc = turn(a, EDGE), turn(c, EDGE)
        before = (jnp.where(lane < EDGE, zero, ra), jnp.where(lane < EDGE, ra, rc))
        ra, rc = turn(a, -EDGE), turn(c, -EDGE)
        after = (jnp.where(edge, rc, ra), jnp.where(edge, zero, rc))
        blocks = []
        for left, right in (before, (a, c), after):
            for l, r in zip(z_shifted(left, zero, zero), z_shifted(right, zero, zero)):
                blocks.append(jnp.concatenate([l, r], axis=1))
        tall = jnp.concatenate(blocks, axis=0)
        dy = 2 * (index % 2)
        rows = matrix[dy * channels : (dy + 1) * channels, :]
        return jnp.dot(rows, tall, preferred_element_type=jnp.float32)

    low_y, high_y = y_face(2), y_face(3)
    for x, index in ((-1, 0), (EDGE, 1)):
        inner = at_x(EDGE - 1 if index == 0 else 0)
        slab = face(index, lambda k, inner=inner: values[k, :, inner], halo_x)
        left = z_shifted(slab[:, :HALF], zero, zero)
        put(stacked, b, x, left, z_shifted(slab[:, HALF:], zero, zero))
    for x in range(EDGE):
        taps = stacked[b, x : x + 3].reshape(9 * channels, SLAB)
        sums = jnp.dot(matrix[...], taps, preferred_element_type=jnp.float32)
        before, middle, after = (sums[i * channels : (i + 1) * channels] for i in range(3))
        plane_half = slice(x // 8 * HALF, (x // 8 + 1) * HALF)
        place = (x % 8) * EDGE
        low = turn(low_y[:, plane_half], -place)
        high = turn(high_y[:, plane_half], HALF - EDGE - place)
        ra, rc = turn(before[:, :HALF], EDGE), turn(before[:, HALF:], EDGE)
        first = (jnp.where(lane < EDGE, low, ra), jnp.where(lane < EDGE, ra, rc))
        ra, rc = turn(after[:, :HALF], -EDGE), turn(after[:, HALF:], -EDGE)
        second = (jnp.where(edge, rc, ra), jnp.where(edge, high, rc))
        for half in range(2):
            total = middle[:, half * HALF : (half + 1) * HALF] + first[half]
            total = total + second[half] + bias[...]
            finish(slice(x * SLAB + half * HALF, x * SLAB + (half + 1) * HALF), total)


def prepare(weights, bias, matrix, column_out):
    channels = weights.shape[1]
    for dy in range(3):
        blocks = [weights[9 * (j // 3) + 3 * dy + j % 3] for j in range(9)]
        rows = slice(dy * channels, (dy + 1) * channels)
        for pair in range(4):
            columns = slice(pair * 2 * channels, (pair + 1) * 2 * channels)
            matrix[rows, columns] = jnp.concatenate(blocks[2 * pair : 2 * pair + 2], axis=1)
        matrix[rows, 8 * channels : 9 * channels] = blocks[8]
    row = lax.broadcasted_iota(jnp.int32, (channels, channels), 0)
    column = lax.broadcasted_iota(jnp.int32, (channels, channels), 1)
    wide = jnp.broadcast_to(bias[...], (channels, channels))
    one = jnp.sum(jnp.where(row == column, wide, 0.0), axis=1, keepdims=True)
    column_out[...] = jnp.broadcast_to(one, (channels, HALF))


def body(
    state, neighbor, features, w_first, b_first, w_second, b_second, out,
    staged, hidden, result, stacked,
    planes_1, halo_x_1, halo_y_1, planes_2, halo_x_2, halo_y_2,
    weights_1, weights_2, matrix_1, matrix_2, bias_1, bias_2,
    load_sem, weight_sem, store_sem, send_sem_1, recv_sem_1, send_sem_2, recv_sem_2,
):
    bricks = staged.shape[0]
    kind = staged.dtype
    n_x, n_y = lax.axis_size("gx"), lax.axis_size("yz")
    gx, yz = lax.axis_index("gx"), lax.axis_index("yz")
    x_up = (lax.rem(gx + 1, n_x), yz)
    x_down = (lax.rem(gx + n_x - 1, n_x), yz)
    y_up = (gx, lax.rem(yz + 1, n_y))
    y_down = (gx, lax.rem(yz + n_y - 1, n_y))
    others = (x_up, x_down, y_up, y_down)

    barrier = pltpu.get_barrier_semaphore()
    for other in others:
        pl.semaphore_signal(barrier, inc=1, device_id=other, device_id_type=MESH)
    load = pltpu.make_async_copy(features, staged, load_sem)
    load.start()
    weight_loads = [
        pltpu.make_async_copy(w_first, weights_1, weight_sem.at[0]),
        pltpu.make_async_copy(w_second, weights_2, weight_sem.at[1]),
    ]
    for copy in weight_loads:
        copy.start()
    pl.semaphore_wait(barrier, 4)

    def remote(src, dst, sems, other):
        return pltpu.make_async_remote_copy(
            src_ref=src,
            dst_ref=dst,
            send_sem=sems[0],
            recv_sem=sems[1],
            device_id=other,
            device_id_type=MESH,
        )

    last = pl.ds((EDGE - 1) * SLAB, SLAB)
    sems_1 = [(send_sem_1.at[i], recv_sem_1.at[i]) for i in range(4)]
    exchange = [
        remote(features.at[:, :, last], halo_x_1.at[0], sems_1[0], x_up),
        remote(features.at[:, :, pl.ds(0, SLAB)], halo_x_1.at[1], sems_1[1], x_down),
        remote(planes_1.at[1], halo_y_1.at[0], sems_1[2], y_up),
        remote(planes_1.at[0], halo_y_1.at[1], sems_1[3], y_down),
    ]
    exchange[0].start()
    exchange[1].start()
    load.wait()

    @pl.loop(0, bricks)
    def _(b):
        outer_rows(staged, b, planes_1)

    exchange[2].start()
    exchange[3].start()
    for copy in weight_loads:
        copy.wait()
    prepare(weights_1, b_first, matrix_1, bias_1)
    prepare(weights_2, b_second, matrix_2, bias_2)

    @pl.loop(0, bricks)
    def _(b):
        stack_brick(staged, neighbor, b, stacked)

    for copy in exchange:
        copy.wait()

    def hidden_copies(b):
        sems = [(send_sem_2.at[i, b], recv_sem_2.at[i, b]) for i in range(4)]
        return [
            remote(hidden.at[b, :, last], halo_x_2.at[0, b], sems[0], x_up),
            remote(hidden.at[b, :, pl.ds(0, SLAB)], halo_x_2.at[1, b], sems[1], x_down),
            remote(planes_2.at[1, b], halo_y_2.at[0, b], sems[2], y_up),
            remote(planes_2.at[0, b], halo_y_2.at[1, b], sems[3], y_down),
        ]

    @pl.loop(0, bricks)
    def _(b):
        live = state[b] >= 0

        def finish(span, total):
            hidden[b, :, span] = jnp.where(live, jnp.maximum(total, 0.0), 0.0).astype(kind)

        conv_brick(
            staged, halo_x_1, halo_y_1, planes_1, neighbor, b, stacked, matrix_1, bias_1, finish
        )
        outer_rows(hidden, b, planes_2)
        for copy in hidden_copies(b):
            copy.start()

    @pl.loop(0, bricks)
    def _(b):
        stack_brick(hidden, neighbor, b, stacked)

    @pl.loop(0, bricks)
    def _(b):
        for copy in hidden_copies(b):
            copy.wait()

    def store(b):
        return pltpu.make_async_copy(result.at[b], out.at[b], store_sem.at[b])

    @pl.loop(0, bricks)
    def _(b):
        live = state[b] >= 0

        def finish(span, total):
            branch = total.astype(kind).astype(jnp.float32)
            summed = staged[b, :, span].astype(jnp.float32) + branch
            result[b, :, span] = jnp.where(live, jnp.maximum(summed, 0.0), 0.0).astype(kind)

        conv_brick(
            hidden, halo_x_2, halo_y_2, planes_2, neighbor, b, stacked, matrix_2, bias_2, finish
        )
        store(b).start()

    @pl.loop(0, bricks)
    def _(b):
        store(b).wait()


def per_device(features, brick_state, neighbor, w_first, b_first, w_second, b_second):
    bricks, channels, _ = features.shape
    kind = features.dtype
    anywhere = pl.BlockSpec(memory_space=pl.ANY)
    whole = pl.BlockSpec(memory_space=VMEM)
    scalar = pl.BlockSpec(memory_space=pltpu.SMEM)
    brick_set = VMEM(features.shape, kind)
    plane_set = VMEM((2, bricks, channels, SLAB), kind)
    matrix = VMEM((3 * channels, 9 * channels), kind)
    column = VMEM((channels, HALF), jnp.float32)
    dma = pltpu.SemaphoreType.DMA
    return pl.pallas_call(
        body,
        out_shape=jax.ShapeDtypeStruct(features.shape, kind),
        in_specs=[scalar, scalar, anywhere, anywhere, whole, anywhere, whole],
        out_specs=anywhere,
        scratch_shapes=[
            brick_set, brick_set, brick_set,
            VMEM((bricks, EDGE + 2, 3 * channels, SLAB), kind),
            *[plane_set] * 6,
            VMEM(w_first.shape, kind), VMEM(w_second.shape, kind),
            matrix, matrix, column, column,
            dma, dma((2,)), dma((bricks,)),
            dma((4,)), dma((4,)), dma((4, bricks)), dma((4, bricks)),
        ],
        compiler_params=pltpu.CompilerParams(
            collective_id=0, has_side_effects=True, vmem_limit_bytes=LIMIT
        ),
        name="residual_pair",
    )(
        brick_state, neighbor, features,
        w_first, b_first.reshape(1, channels), w_second, b_second.reshape(1, channels),
    )


def solution(mesh):
    in_specs = (
        P(("gx", "yz"), None, None),
        P(("gx", "yz")),
        P(("gx", "yz"), None),
        P(),
        P(),
        P(),
        P(),
    )
    out_specs = P(("gx", "yz"), None, None)
    return jax.shard_map(
        per_device, mesh=mesh, in_specs=in_specs, out_specs=out_specs, check_vma=False
    )
```

```python
import jax
import jax.numpy as jnp
from jax import lax
from jax.experimental import pallas as pl
from jax.experimental.pallas import tpu as pltpu
from jax.sharding import PartitionSpec as P

EDGE = 16
SLAB = EDGE * EDGE
HALF = SLAB // 2
MESH = pl.DeviceIdType.MESH
VMEM = pltpu.VMEM
LIMIT = 58 * 2**20


def lanes(rows):
    return lax.broadcasted_iota(jnp.int32, (rows, HALF), 1)


def turn(values, shift):
    shift = shift % HALF
    return values if shift == 0 else pltpu.roll(values, shift, axis=1)


def gather_row(plane, slab_half, x, source_lane):
    place = (x % 8) * EDGE
    lane = lanes(plane.shape[0])
    inside = (lane >= place) & (lane < place + EDGE)
    return jnp.where(inside, turn(slab_half, place - source_lane), plane)


def at_x(x):
    return slice(x * SLAB, (x + 1) * SLAB)


def outer_rows(values, b, planes):
    channels = values.shape[1]
    for half in range(2):
        low = jnp.zeros((channels, HALF), values.dtype)
        high = low
        for x in range(half * 8, half * 8 + 8):
            low = gather_row(low, values[b, :, x * SLAB : x * SLAB + HALF], x, 0)
            high = gather_row(high, values[b, :, x * SLAB + HALF : (x + 1) * SLAB], x, HALF - EDGE)
        planes[0, b, :, half * HALF : (half + 1) * HALF] = low
        planes[1, b, :, half * HALF : (half + 1) * HALF] = high


def z_shifted(half, below, above):
    z = lanes(half.shape[0]) % EDGE
    down = jnp.where(z == 0, below, turn(half, 1))
    up = jnp.where(z == EDGE - 1, above, turn(half, -1))
    return down, half, up


def put(stacked, b, x, left, right):
    channels = left[0].shape[0]
    for dz in range(3):
        rows = slice(dz * channels, (dz + 1) * channels)
        stacked[b, x + 1, rows, :HALF] = left[dz]
        stacked[b, x + 1, rows, HALF:] = right[dz]


def stack_brick(values, neighbor, b, stacked):
    bricks, channels = values.shape[0], values.shape[1]
    zero = jnp.zeros((channels, HALF), values.dtype)

    def z_neighbor(index):
        k = neighbor[b, index]
        return k >= 0, jnp.clip(jnp.where(k >= bricks, k - bricks, k), 0, bricks - 1)

    has_below, below = z_neighbor(4)
    has_above, above = z_neighbor(5)
    for x in range(EDGE):
        shifts = []
        for half in range(2):
            span = slice(x * SLAB + half * HALF, x * SLAB + (half + 1) * HALF)
            low = turn(values[below, :, span], 1 - EDGE)
            high = turn(values[above, :, span], EDGE - 1)
            shifts.append(
                z_shifted(
                    values[b, :, span],
                    jnp.where(has_below, low, zero),
                    jnp.where(has_above, high, zero),
                )
            )
        put(stacked, b, x, *shifts)


def conv_brick(values, halo_x, halo_y, own_y, neighbor, b, stacked, matrix, bias, finish):
    bricks, channels = values.shape[0], values.shape[1]
    lane = lanes(channels)
    zero = jnp.zeros((channels, HALF), values.dtype)
    edge = lane >= HALF - EDGE

    def face(index, own, across):
        k = neighbor[b, index]
        here = jnp.clip(k, 0, bricks - 1)
        there = jnp.clip(k - bricks, 0, bricks - 1)
        picked = jnp.where(k < bricks, own(here), across[index % 2, there])
        return jnp.where(k >= 0, picked, jnp.zeros_like(picked))

    def y_face(index):
        plane = face(index, lambda k: own_y[1 - index % 2, k], halo_y)
        a, c = plane[:, :HALF], plane[:, HALF:]
        ra, rc = turn(a, EDGE), turn(c, EDGE)
        before = (jnp.where(lane < EDGE, zero, ra), jnp.where(lane < EDGE, ra, rc))
        ra, rc = turn(a, -EDGE), turn(c, -EDGE)
        after = (jnp.where(edge, rc, ra), jnp.where(edge, zero, rc))
        blocks = []
        for left, right in (before, (a, c), after):
            for l, r in zip(z_shifted(left, zero, zero), z_shifted(right, zero, zero)):
                blocks.append(jnp.concatenate([l, r], axis=1))
        tall = jnp.concatenate(blocks, axis=0)
        dy = 2 * (index % 2)
        rows = matrix[dy * channels : (dy + 1) * channels, :]
        return jnp.dot(rows, tall, preferred_element_type=jnp.float32)

    low_y, high_y = y_face(2), y_face(3)
    for x, index in ((-1, 0), (EDGE, 1)):
        inner = at_x(EDGE - 1 if index == 0 else 0)
        slab = face(index, lambda k, inner=inner: values[k, :, inner], halo_x)
        left = z_shifted(slab[:, :HALF], zero, zero)
        put(stacked, b, x, left, z_shifted(slab[:, HALF:], zero, zero))
    for x in range(EDGE):
        taps = stacked[b, x : x + 3].reshape(9 * channels, SLAB)
        sums = jnp.dot(matrix[...], taps, preferred_element_type=jnp.float32)
        before, middle, after = (sums[i * channels : (i + 1) * channels] for i in range(3))
        plane_half = slice(x // 8 * HALF, (x // 8 + 1) * HALF)
        place = (x % 8) * EDGE
        low = turn(low_y[:, plane_half], -place)
        high = turn(high_y[:, plane_half], HALF - EDGE - place)
        ra, rc = turn(before[:, :HALF], EDGE), turn(before[:, HALF:], EDGE)
        first = (jnp.where(lane < EDGE, low, ra), jnp.where(lane < EDGE, ra, rc))
        ra, rc = turn(after[:, :HALF], -EDGE), turn(after[:, HALF:], -EDGE)
        second = (jnp.where(edge, rc, ra), jnp.where(edge, high, rc))
        for half in range(2):
            total = middle[:, half * HALF : (half + 1) * HALF] + first[half]
            total = total + second[half] + bias[...]
            finish(slice(x * SLAB + half * HALF, x * SLAB + (half + 1) * HALF), total)


def prepare(weights, bias, matrix, column_out):
    channels = weights.shape[1]
    for dy in range(3):
        blocks = [weights[9 * (j // 3) + 3 * dy + j % 3] for j in range(9)]
        rows = slice(dy * channels, (dy + 1) * channels)
        for pair in range(4):
            columns = slice(pair * 2 * channels, (pair + 1) * 2 * channels)
            matrix[rows, columns] = jnp.concatenate(blocks[2 * pair : 2 * pair + 2], axis=1)
        matrix[rows, 8 * channels : 9 * channels] = blocks[8]
    row = lax.broadcasted_iota(jnp.int32, (channels, channels), 0)
    column = lax.broadcasted_iota(jnp.int32, (channels, channels), 1)
    wide = jnp.broadcast_to(bias[...], (channels, channels))
    one = jnp.sum(jnp.where(row == column, wide, 0.0), axis=1, keepdims=True)
    column_out[...] = jnp.broadcast_to(one, (channels, HALF))


def body(
    state, neighbor, features, w_first, b_first, w_second, b_second, out,
    staged, hidden, stacked,
    planes_1, halo_x_1, halo_y_1, planes_2, halo_x_2, halo_y_2,
    weights_1, weights_2, matrix_1, matrix_2, bias_1, bias_2,
    load_sem, weight_sem, send_x, recv_x, send_sem_1, recv_sem_1, send_sem_2, recv_sem_2,
):
    bricks = staged.shape[0]
    kind = staged.dtype
    n_x, n_y = lax.axis_size("gx"), lax.axis_size("yz")
    gx, yz = lax.axis_index("gx"), lax.axis_index("yz")
    x_up = (lax.rem(gx + 1, n_x), yz)
    x_down = (lax.rem(gx + n_x - 1, n_x), yz)
    y_up = (gx, lax.rem(yz + 1, n_y))
    y_down = (gx, lax.rem(yz + n_y - 1, n_y))
    others = (x_up, x_down, y_up, y_down)

    barrier = pltpu.get_barrier_semaphore()
    for other in others:
        pl.semaphore_signal(barrier, inc=1, device_id=other, device_id_type=MESH)

    def load(b):
        return pltpu.make_async_copy(features.at[b], staged.at[b], load_sem.at[b])

    for b in range(bricks):
        load(b).start()
    weight_loads = [
        pltpu.make_async_copy(w_first, weights_1, weight_sem.at[0]),
        pltpu.make_async_copy(w_second, weights_2, weight_sem.at[1]),
    ]
    for copy in weight_loads:
        copy.start()
    pl.semaphore_wait(barrier, 4)

    def remote(src, dst, sems, other):
        return pltpu.make_async_remote_copy(
            src_ref=src,
            dst_ref=dst,
            send_sem=sems[0],
            recv_sem=sems[1],
            device_id=other,
            device_id_type=MESH,
        )

    last = pl.ds((EDGE - 1) * SLAB, SLAB)
    across_x = [
        remote(features.at[:, :, last], halo_x_1.at[0], (send_x.at[0], recv_x.at[0]), x_up),
        remote(
            features.at[:, :, pl.ds(0, SLAB)], halo_x_1.at[1], (send_x.at[1], recv_x.at[1]), x_down
        ),
    ]

    def across_y(b):
        sems = [(send_sem_1.at[i, b], recv_sem_1.at[i, b]) for i in range(2)]
        return [
            remote(planes_1.at[1, b], halo_y_1.at[0, b], sems[0], y_up),
            remote(planes_1.at[0, b], halo_y_1.at[1, b], sems[1], y_down),
        ]

    for copy in across_x:
        copy.start()

    @pl.loop(0, bricks)
    def _(b):
        load(b).wait()
        outer_rows(staged, b, planes_1)
        for copy in across_y(b):
            copy.start()

    for copy in weight_loads:
        copy.wait()
    prepare(weights_1, b_first, matrix_1, bias_1)
    prepare(weights_2, b_second, matrix_2, bias_2)

    @pl.loop(0, bricks)
    def _(b):
        stack_brick(staged, neighbor, b, stacked)

    for copy in across_x:
        copy.wait()

    @pl.loop(0, bricks)
    def _(b):
        for copy in across_y(b):
            copy.wait()

    def hidden_copies(b):
        sems = [(send_sem_2.at[i, b], recv_sem_2.at[i, b]) for i in range(4)]
        return [
            remote(hidden.at[b, :, last], halo_x_2.at[0, b], sems[0], x_up),
            remote(hidden.at[b, :, pl.ds(0, SLAB)], halo_x_2.at[1, b], sems[1], x_down),
            remote(planes_2.at[1, b], halo_y_2.at[0, b], sems[2], y_up),
            remote(planes_2.at[0, b], halo_y_2.at[1, b], sems[3], y_down),
        ]

    @pl.loop(0, bricks)
    def _(b):
        live = state[b] >= 0

        def finish(span, total):
            hidden[b, :, span] = jnp.where(live, jnp.maximum(total, 0.0), 0.0).astype(kind)

        conv_brick(
            staged, halo_x_1, halo_y_1, planes_1, neighbor, b, stacked, matrix_1, bias_1, finish
        )
        outer_rows(hidden, b, planes_2)
        for copy in hidden_copies(b):
            copy.start()

    @pl.loop(0, bricks)
    def _(b):
        stack_brick(hidden, neighbor, b, stacked)

    @pl.loop(0, bricks)
    def _(b):
        for copy in hidden_copies(b):
            copy.wait()

    @pl.loop(0, bricks)
    def _(b):
        live = state[b] >= 0

        def finish(span, total):
            branch = total.astype(kind).astype(jnp.float32)
            summed = staged[b, :, span].astype(jnp.float32) + branch
            out[b, :, span] = jnp.where(live, jnp.maximum(summed, 0.0), 0.0).astype(kind)

        conv_brick(
            hidden, halo_x_2, halo_y_2, planes_2, neighbor, b, stacked, matrix_2, bias_2, finish
        )


def store_body(blocks, out, sem):
    copies = [
        pltpu.make_async_copy(blocks.at[b], out.at[b], sem.at[b]) for b in range(blocks.shape[0])
    ]
    for copy in copies:
        copy.start()
    for copy in copies:
        copy.wait()


def per_device(features, brick_state, neighbor, w_first, b_first, w_second, b_second):
    bricks, channels, _ = features.shape
    kind = features.dtype
    anywhere = pl.BlockSpec(memory_space=pl.ANY)
    whole = pl.BlockSpec(memory_space=VMEM)
    scalar = pl.BlockSpec(memory_space=pltpu.SMEM)
    brick_set = VMEM(features.shape, kind)
    plane_set = VMEM((2, bricks, channels, SLAB), kind)
    matrix = VMEM((3 * channels, 9 * channels), kind)
    column = VMEM((channels, HALF), jnp.float32)
    dma = pltpu.SemaphoreType.DMA
    blocks = pl.pallas_call(
        body,
        out_shape=VMEM(features.shape, kind),
        in_specs=[scalar, scalar, anywhere, anywhere, whole, anywhere, whole],
        out_specs=whole,
        scratch_shapes=[
            brick_set, brick_set,
            VMEM((bricks, EDGE + 2, 3 * channels, SLAB), kind),
            *[plane_set] * 6,
            VMEM(w_first.shape, kind), VMEM(w_second.shape, kind),
            matrix, matrix, column, column,
            dma((bricks,)), dma((2,)), dma((2,)), dma((2,)),
            dma((2, bricks)), dma((2, bricks)), dma((4, bricks)), dma((4, bricks)),
        ],
        compiler_params=pltpu.CompilerParams(
            collective_id=0, has_side_effects=True, vmem_limit_bytes=LIMIT
        ),
        name="residual_pair",
    )(
        brick_state, neighbor, features,
        w_first, b_first.reshape(1, channels), w_second, b_second.reshape(1, channels),
    )
    return pl.pallas_call(
        store_body,
        out_shape=jax.ShapeDtypeStruct(features.shape, kind),
        in_specs=[whole],
        out_specs=anywhere,
        scratch_shapes=[dma((bricks,))],
        compiler_params=pltpu.CompilerParams(vmem_limit_bytes=16 * 2**20),
        name="store_blocks",
    )(blocks)


def solution(mesh):
    in_specs = (
        P(("gx", "yz"), None, None),
        P(("gx", "yz")),
        P(("gx", "yz"), None),
        P(),
        P(),
        P(),
        P(),
    )
    out_specs = P(("gx", "yz"), None, None)
    return jax.shard_map(
        per_device, mesh=mesh, in_specs=in_specs, out_specs=out_specs, check_vma=False
    )
```

```python
import jax
import jax.numpy as jnp
from jax import lax
from jax.experimental import pallas as pl
from jax.experimental.pallas import tpu as pltpu
from jax.sharding import PartitionSpec as P

EDGE = 16
SLAB = EDGE * EDGE
HALF = SLAB // 2
MESH = pl.DeviceIdType.MESH
VMEM = pltpu.VMEM
LIMIT = 58 * 2**20


def lanes(rows):
    return lax.broadcasted_iota(jnp.int32, (rows, HALF), 1)


def turn(values, shift):
    shift = shift % HALF
    return values if shift == 0 else pltpu.roll(values, shift, axis=1)


def gather_row(plane, slab_half, x, source_lane):
    place = (x % 8) * EDGE
    lane = lanes(plane.shape[0])
    inside = (lane >= place) & (lane < place + EDGE)
    return jnp.where(inside, turn(slab_half, place - source_lane), plane)


def at_x(x):
    return slice(x * SLAB, (x + 1) * SLAB)


def outer_rows(values, b, planes):
    channels = values.shape[1]
    for half in range(2):
        low = jnp.zeros((channels, HALF), values.dtype)
        high = low
        for x in range(half * 8, half * 8 + 8):
            low = gather_row(low, values[b, :, x * SLAB : x * SLAB + HALF], x, 0)
            high = gather_row(high, values[b, :, x * SLAB + HALF : (x + 1) * SLAB], x, HALF - EDGE)
        planes[0, b, :, half * HALF : (half + 1) * HALF] = low
        planes[1, b, :, half * HALF : (half + 1) * HALF] = high


def z_shifted(half, below, above):
    z = lanes(half.shape[0]) % EDGE
    down = jnp.where(z == 0, below, turn(half, 1))
    up = jnp.where(z == EDGE - 1, above, turn(half, -1))
    return down, half, up


def stack_brick(values, neighbor, b, stacked):
    bricks, channels = values.shape[0], values.shape[1]
    zero = jnp.zeros((channels, HALF), values.dtype)

    def z_neighbor(index):
        k = neighbor[b, index]
        return k >= 0, jnp.clip(jnp.where(k >= bricks, k - bricks, k), 0, bricks - 1)

    has_below, below = z_neighbor(4)
    has_above, above = z_neighbor(5)

    def shifts(x, half):
        span = slice(x * SLAB + half * HALF, x * SLAB + (half + 1) * HALF)
        low = turn(values[below, :, span], 1 - EDGE)
        high = turn(values[above, :, span], EDGE - 1)
        return z_shifted(
            values[b, :, span],
            jnp.where(has_below, low, zero),
            jnp.where(has_above, high, zero),
        )

    for half in range(2):
        columns = slice(half * HALF, (half + 1) * HALF)
        before, first = None, shifts(0, half)
        for pair in range(EDGE // 2):
            second = shifts(2 * pair + 1, half)
            after = shifts(2 * pair + 2, half) if pair < EDGE // 2 - 1 else None
            for dz in range(3):
                rows = slice(dz * channels, (dz + 1) * channels)
                d1, d2 = first[dz], second[dz]
                stacked[b, pair, 0, rows, columns] = -d2 if before is None else before[dz] - d2
                stacked[b, pair, 1, rows, columns] = d1 + d2
                stacked[b, pair, 2, rows, columns] = d2 - d1
                stacked[b, pair, 3, rows, columns] = d1 if after is None else d1 - after[dz]
            before, first = second, after


def conv_brick(values, halo_x, halo_y, own_y, neighbor, b, stacked, matrix, factors, bias, finish):
    bricks, channels = values.shape[0], values.shape[1]
    lane = lanes(channels)
    zero = jnp.zeros((channels, HALF), values.dtype)
    edge = lane >= HALF - EDGE

    def face(index, own, across):
        k = neighbor[b, index]
        here = jnp.clip(k, 0, bricks - 1)
        there = jnp.clip(k - bricks, 0, bricks - 1)
        picked = jnp.where(k < bricks, own(here), across[index % 2, there])
        return jnp.where(k >= 0, picked, jnp.zeros_like(picked))

    def y_face(index):
        plane = face(index, lambda k: own_y[1 - index % 2, k], halo_y)
        a, c = plane[:, :HALF], plane[:, HALF:]
        ra, rc = turn(a, EDGE), turn(c, EDGE)
        before = (jnp.where(lane < EDGE, zero, ra), jnp.where(lane < EDGE, ra, rc))
        ra, rc = turn(a, -EDGE), turn(c, -EDGE)
        after = (jnp.where(edge, rc, ra), jnp.where(edge, zero, rc))
        blocks = []
        for left, right in (before, (a, c), after):
            for l, r in zip(z_shifted(left, zero, zero), z_shifted(right, zero, zero)):
                blocks.append(jnp.concatenate([l, r], axis=1))
        tall = jnp.concatenate(blocks, axis=0)
        dy = 2 * (index % 2)
        rows = matrix[dy * channels : (dy + 1) * channels, :]
        return jnp.dot(rows, tall, preferred_element_type=jnp.float32)

    low_y, high_y = y_face(2), y_face(3)
    for index, pair, part in ((0, 0, 0), (1, EDGE // 2 - 1, 3)):
        inner = at_x(EDGE - 1 if index == 0 else 0)
        slab = face(index, lambda k, inner=inner: values[k, :, inner], halo_x)
        for half in range(2):
            columns = slice(half * HALF, (half + 1) * HALF)
            for dz, shifted in enumerate(z_shifted(slab[:, columns], zero, zero)):
                rows = slice(dz * channels, (dz + 1) * channels)
                if index == 0:
                    stacked[b, pair, part, rows, columns] += shifted
                else:
                    stacked[b, pair, part, rows, columns] -= shifted
    for x in range(EDGE):
        if x % 2 == 0:
            m = [
                jnp.dot(factors[j], stacked[b, x // 2, j], preferred_element_type=jnp.float32)
                for j in range(4)
            ]
            two = (m[0] + m[1] + m[2], m[1] - m[2] - m[3])
        sums = two[x % 2]
        before, middle, after = (sums[i * channels : (i + 1) * channels] for i in range(3))
        plane_half = slice(x // 8 * HALF, (x // 8 + 1) * HALF)
        place = (x % 8) * EDGE
        low = turn(low_y[:, plane_half], -place)
        high = turn(high_y[:, plane_half], HALF - EDGE - place)
        ra, rc = turn(before[:, :HALF], EDGE), turn(before[:, HALF:], EDGE)
        first = (jnp.where(lane < EDGE, low, ra), jnp.where(lane < EDGE, ra, rc))
        ra, rc = turn(after[:, :HALF], -EDGE), turn(after[:, HALF:], -EDGE)
        second = (jnp.where(edge, rc, ra), jnp.where(edge, high, rc))
        for half in range(2):
            total = middle[:, half * HALF : (half + 1) * HALF] + first[half]
            total = total + second[half] + bias[...]
            finish(slice(x * SLAB + half * HALF, x * SLAB + (half + 1) * HALF), total)


def prepare(weights, bias, matrix, factors, column_out):
    channels = weights.shape[1]
    for dy in range(3):
        blocks = [weights[9 * (j // 3) + 3 * dy + j % 3] for j in range(9)]
        rows = slice(dy * channels, (dy + 1) * channels)
        for pair in range(4):
            columns = slice(pair * 2 * channels, (pair + 1) * 2 * channels)
            matrix[rows, columns] = jnp.concatenate(blocks[2 * pair : 2 * pair + 2], axis=1)
        matrix[rows, 8 * channels : 9 * channels] = blocks[8]
    for dy in range(3):
        rows = slice(dy * channels, (dy + 1) * channels)
        for dz in range(3):
            g0, g1, g2 = (weights[9 * dx + 3 * dy + dz].astype(jnp.float32) for dx in range(3))
            columns = slice(dz * channels, (dz + 1) * channels)
            for j, g in enumerate((g0, 0.5 * (g0 + g1 + g2), 0.5 * (g0 - g1 + g2), g2)):
                factors[j, rows, columns] = g.astype(weights.dtype)
    row = lax.broadcasted_iota(jnp.int32, (channels, channels), 0)
    column = lax.broadcasted_iota(jnp.int32, (channels, channels), 1)
    wide = jnp.broadcast_to(bias[...], (channels, channels))
    one = jnp.sum(jnp.where(row == column, wide, 0.0), axis=1, keepdims=True)
    column_out[...] = jnp.broadcast_to(one, (channels, HALF))


def body(
    state, neighbor, features, w_first, b_first, w_second, b_second, out,
    staged, hidden, stacked,
    planes_1, halo_x_1, halo_y_1, planes_2, halo_x_2, halo_y_2,
    weights_1, weights_2, matrix_1, matrix_2, factors_1, factors_2, bias_1, bias_2,
    load_sem, weight_sem, send_x, recv_x, send_sem_1, recv_sem_1, send_sem_2, recv_sem_2,
):
    bricks = staged.shape[0]
    kind = staged.dtype
    n_x, n_y = lax.axis_size("gx"), lax.axis_size("yz")
    gx, yz = lax.axis_index("gx"), lax.axis_index("yz")
    x_up = (lax.rem(gx + 1, n_x), yz)
    x_down = (lax.rem(gx + n_x - 1, n_x), yz)
    y_up = (gx, lax.rem(yz + 1, n_y))
    y_down = (gx, lax.rem(yz + n_y - 1, n_y))
    others = (x_up, x_down, y_up, y_down)

    barrier = pltpu.get_barrier_semaphore()
    for other in others:
        pl.semaphore_signal(barrier, inc=1, device_id=other, device_id_type=MESH)

    def load(b):
        return pltpu.make_async_copy(features.at[b], staged.at[b], load_sem.at[b])

    for b in range(bricks):
        load(b).start()
    weight_loads = [
        pltpu.make_async_copy(w_first, weights_1, weight_sem.at[0]),
        pltpu.make_async_copy(w_second, weights_2, weight_sem.at[1]),
    ]
    for copy in weight_loads:
        copy.start()
    pl.semaphore_wait(barrier, 4)

    def remote(src, dst, sems, other):
        return pltpu.make_async_remote_copy(
            src_ref=src,
            dst_ref=dst,
            send_sem=sems[0],
            recv_sem=sems[1],
            device_id=other,
            device_id_type=MESH,
        )

    last = pl.ds((EDGE - 1) * SLAB, SLAB)
    across_x = [
        remote(features.at[:, :, last], halo_x_1.at[0], (send_x.at[0], recv_x.at[0]), x_up),
        remote(
            features.at[:, :, pl.ds(0, SLAB)], halo_x_1.at[1], (send_x.at[1], recv_x.at[1]), x_down
        ),
    ]

    def across_y(b):
        sems = [(send_sem_1.at[i, b], recv_sem_1.at[i, b]) for i in range(2)]
        return [
            remote(planes_1.at[1, b], halo_y_1.at[0, b], sems[0], y_up),
            remote(planes_1.at[0, b], halo_y_1.at[1, b], sems[1], y_down),
        ]

    for copy in across_x:
        copy.start()

    @pl.loop(0, bricks)
    def _(b):
        load(b).wait()
        outer_rows(staged, b, planes_1)
        for copy in across_y(b):
            copy.start()

    for copy in weight_loads:
        copy.wait()
    prepare(weights_1, b_first, matrix_1, factors_1, bias_1)
    prepare(weights_2, b_second, matrix_2, factors_2, bias_2)

    @pl.loop(0, bricks)
    def _(b):
        stack_brick(staged, neighbor, b, stacked)

    for copy in across_x:
        copy.wait()

    @pl.loop(0, bricks)
    def _(b):
        for copy in across_y(b):
            copy.wait()

    def hidden_copies(b):
        sems = [(send_sem_2.at[i, b], recv_sem_2.at[i, b]) for i in range(4)]
        return [
            remote(hidden.at[b, :, last], halo_x_2.at[0, b], sems[0], x_up),
            remote(hidden.at[b, :, pl.ds(0, SLAB)], halo_x_2.at[1, b], sems[1], x_down),
            remote(planes_2.at[1, b], halo_y_2.at[0, b], sems[2], y_up),
            remote(planes_2.at[0, b], halo_y_2.at[1, b], sems[3], y_down),
        ]

    @pl.loop(0, bricks)
    def _(b):
        live = state[b] >= 0

        def finish(span, total):
            hidden[b, :, span] = jnp.where(live, jnp.maximum(total, 0.0), 0.0).astype(kind)

        conv_brick(
            staged, halo_x_1, halo_y_1, planes_1, neighbor, b, stacked, matrix_1, factors_1, bias_1, finish
        )
        outer_rows(hidden, b, planes_2)
        for copy in hidden_copies(b):
            copy.start()

    @pl.loop(0, bricks)
    def _(b):
        stack_brick(hidden, neighbor, b, stacked)

    @pl.loop(0, bricks)
    def _(b):
        for copy in hidden_copies(b):
            copy.wait()

    @pl.loop(0, bricks)
    def _(b):
        live = state[b] >= 0

        def finish(span, total):
            branch = total.astype(kind).astype(jnp.float32)
            summed = staged[b, :, span].astype(jnp.float32) + branch
            out[b, :, span] = jnp.where(live, jnp.maximum(summed, 0.0), 0.0).astype(kind)

        conv_brick(
            hidden, halo_x_2, halo_y_2, planes_2, neighbor, b, stacked, matrix_2, factors_2, bias_2, finish
        )


def store_body(blocks, out, sem):
    copies = [
        pltpu.make_async_copy(blocks.at[b], out.at[b], sem.at[b]) for b in range(blocks.shape[0])
    ]
    for copy in copies:
        copy.start()
    for copy in copies:
        copy.wait()


def per_device(features, brick_state, neighbor, w_first, b_first, w_second, b_second):
    bricks, channels, _ = features.shape
    kind = features.dtype
    anywhere = pl.BlockSpec(memory_space=pl.ANY)
    whole = pl.BlockSpec(memory_space=VMEM)
    scalar = pl.BlockSpec(memory_space=pltpu.SMEM)
    brick_set = VMEM(features.shape, kind)
    plane_set = VMEM((2, bricks, channels, SLAB), kind)
    matrix = VMEM((3 * channels, 9 * channels), kind)
    factors = VMEM((4, 3 * channels, 3 * channels), kind)
    column = VMEM((channels, HALF), jnp.float32)
    dma = pltpu.SemaphoreType.DMA
    blocks = pl.pallas_call(
        body,
        out_shape=VMEM(features.shape, kind),
        in_specs=[scalar, scalar, anywhere, anywhere, whole, anywhere, whole],
        out_specs=whole,
        scratch_shapes=[
            brick_set, brick_set,
            VMEM((bricks, EDGE // 2, 4, 3 * channels, SLAB), kind),
            *[plane_set] * 6,
            VMEM(w_first.shape, kind), VMEM(w_second.shape, kind),
            matrix, matrix, factors, factors, column, column,
            dma((bricks,)), dma((2,)), dma((2,)), dma((2,)),
            dma((2, bricks)), dma((2, bricks)), dma((4, bricks)), dma((4, bricks)),
        ],
        compiler_params=pltpu.CompilerParams(
            collective_id=0, has_side_effects=True, vmem_limit_bytes=LIMIT
        ),
        name="residual_pair",
    )(
        brick_state, neighbor, features,
        w_first, b_first.reshape(1, channels), w_second, b_second.reshape(1, channels),
    )
    return pl.pallas_call(
        store_body,
        out_shape=jax.ShapeDtypeStruct(features.shape, kind),
        in_specs=[whole],
        out_specs=anywhere,
        scratch_shapes=[dma((bricks,))],
        compiler_params=pltpu.CompilerParams(vmem_limit_bytes=16 * 2**20),
        name="store_blocks",
    )(blocks)


def solution(mesh):
    in_specs = (
        P(("gx", "yz"), None, None),
        P(("gx", "yz")),
        P(("gx", "yz"), None),
        P(),
        P(),
        P(),
        P(),
    )
    out_specs = P(("gx", "yz"), None, None)
    return jax.shard_map(
        per_device, mesh=mesh, in_specs=in_specs, out_specs=out_specs, check_vma=False
    )
```
